32 devices in a mesh: ctx: 8 (over z, core), exp: 4 (over y, x).
Axes of the slice: x: 2, y: 2, z: 4, core: 2. Of those that a mesh axis runs over, the one named last changes fastest.
Arguments:
- x_inner: bfloat16 [2048, 4096], P('ctx', 'exp'), may hold values from -6 to 6
- bc_input: bfloat16 [2048, 256], P('ctx'), may hold values from -6 to 6
- gate_input: bfloat16 [2048, 4096], P('ctx', 'exp'), may hold values from -22 to 22
- conv_weight: float32 [4, 4096], P(None, 'exp'), may hold values from -3 to 3
- bc_conv_weight: float32 [4, 256], replicated, may hold values from -3 to 3
- step_size: float32 [2048, 64], P('ctx', 'exp'), may hold values from 0.002 to 0.05
- log_decay: float32 [2048, 64], P('ctx', 'exp'), may hold values from -1 to 0
- skip_gain: float32 [64], P('exp'), may hold values from 0.5 to 1.5
- norm_gain: float32 [4096], P('exp'), may hold values from 0.25 to 1.75
- out_weight: bfloat16 [4096, 2048], P('exp'), may hold values from -0.09375 to 0.09375
- residual: bfloat16 [2048, 2048], P(('ctx', 'exp')), may hold values from -6 to 6
- moe_gain: float32 [2048], replicated, may hold values from 0.25 to 1.75
- expert_ids: int32 [2048, 4], P(('ctx', 'exp')), may hold values from 0 to 7, all different within a row; in each aligned block of 64 rows (0 to 63, 64 to 127, ...) at most 36 rows name the same one
- route_weights: float32 [2048, 4], P(('ctx', 'exp')), may hold values from 0.1 to 0.6
- gate_up_weight: bfloat16 [8, 2048, 1408], P('exp', 'ctx'), may hold values from -0.125 to 0.125
- down_weight: bfloat16 [8, 704, 2048], P('exp', None, 'ctx'), may hold values from -0.21875 to 0.21875
- out_grad: bfloat16 [2048, 2048], P(('ctx', 'exp')), may hold values from -6 to 6
Outputs:
- layer_output: bfloat16 [2048, 2048], P(('ctx', 'exp'))
- residual_grad: bfloat16 [2048, 2048], P(('ctx', 'exp'))
- route_grads: float32 [2048, 4], P(('ctx', 'exp'))
The draws below stay inside these ranges and needn't reach their ends.
Inputs may be any that keep to these rules, and one draw needn't show every extreme that they name: `expert_ids`: within the rows of one device (aligned blocks of 64 tokens) no expert is named by more than 36 rows, a bound that some block reaches; each row names 4 different experts.
All inputs are finite; a program needn't handle non-finite values.
Results may differ from the reference program's by a relative error of at most 0.03.
Values may be sent and summed in bfloat16 or wider, within the bound.
A program may use at most 128 MiB of HBM per device.

```python
import math
import jax
import jax.numpy as jnp
import numpy as np
from jax import lax

D = 2048
HEADS = 64
HEAD_DIM = 64
STATE = 128
KERNEL = 4
SPAN = 128
MOE_FF = 704
TOP = 4
TOK_DEV = 64
INNER = 4096
ROWS_DEV = 256
SEQUENCE_TOKENS = 2048
EXPERTS = 8
CAP = 36
N_EXP = 4


def draw_log_decay(key, part):
    random_subkeys = jax.random.split(key, 7)
    head_order = jax.random.permutation(random_subkeys[0], HEADS)
    slow_heads = head_order < HEADS // 2
    slow_rate = jnp.exp(jax.random.uniform(random_subkeys[1], (HEADS,), jnp.float32, jnp.log(0.1 / SEQUENCE_TOKENS), jnp.log(1.0 / SEQUENCE_TOKENS)))
    fast_rate = jnp.exp(jax.random.uniform(random_subkeys[2], (HEADS,), jnp.float32, jnp.log(1.0 / 50.0), jnp.log(1.0 / 30.0)))
    head_decay_rate = jnp.where(slow_heads, slow_rate, fast_rate)
    coarse_multiplier = jax.random.uniform(random_subkeys[3], (SEQUENCE_TOKENS, HEADS), jnp.float32, 0.5, 1.5)
    segments = SEQUENCE_TOKENS // ROWS_DEV
    device_multiplier = jnp.exp(jax.random.uniform(random_subkeys[4], (segments, HEADS), jnp.float32, -0.7, 0.7))
    device_multiplier = jnp.repeat(device_multiplier, ROWS_DEV, axis=0)
    spike_groups = jax.random.uniform(random_subkeys[5], (SEQUENCE_TOKENS, 1), jnp.float32) < 3.0 / SEQUENCE_TOKENS
    spike_loss_value = jnp.log(jax.random.uniform(random_subkeys[6], (SEQUENCE_TOKENS, 1), jnp.float32, 0.5, 0.8))
    return -head_decay_rate[None, :] * coarse_multiplier * device_multiplier + jnp.where(spike_groups, spike_loss_value, 0.0)


def draw_gate_input(key, part):
    random_subkeys = jax.random.split(key, 2)
    channel_ramp = jnp.exp(jnp.log(3.0) * jnp.arange(INNER, dtype=jnp.float32) / (INNER - 1))
    jitter = jax.random.uniform(random_subkeys[1], (INNER,), jnp.float32, 0.6, 1.4)
    base_values = jnp.clip(jax.random.normal(random_subkeys[0], (SEQUENCE_TOKENS, INNER), jnp.float32), -5.0, 5.0)
    return (base_values * (channel_ramp * jitter)[None, :]).astype(jnp.bfloat16)


def levels(key, extent, shards, smallest, high):
    level = 1.0
    for position, parts in shards:
        draws = jax.random.uniform(jax.random.fold_in(jax.random.fold_in(key, 6), position), (parts,), jnp.float32, smallest / len(shards), high / len(shards))
        level = level * jnp.repeat(jnp.exp(draws), extent[position] // parts).reshape((-1,) + (1,) * (len(extent) - 1 - position))
    return level


def shared_out(rng, own, number, rows, amount, top, bound, lean):
    ranking = jax.random.permutation(rng, amount)
    packed, ordinary = load_shares(amount, rows * top, bound, lean, True), load_shares(amount, rows * top, bound, lean, False)
    places = jnp.arange(amount)

    def named(sizes, turn):
        used = int((sizes > 0).sum())
        fixed = max(1, used // 4)
        passed = fixed + (places - fixed + turn * (used - fixed)) % max(1, amount - fixed)
        return jnp.zeros((amount,), jnp.int32).at[ranking[jnp.where(places < fixed, places, passed)]].set(jnp.asarray(sizes, jnp.int32))

    sizes = jnp.where(number % 4 == 0, named(packed, number // 4), named(ordinary, number - number // 4 - 1))
    mixed = jax.random.permutation(jax.random.fold_in(own, 3), amount)
    giver, taker = mixed[0:amount // 2 * 2:2], mixed[1:amount // 2 * 2:2]
    room = jnp.minimum(sizes[giver] - 1, bound - sizes[taker]) // 2
    room = jnp.where((giver == ranking[0]) | (taker == ranking[0]) | (sizes[taker] == 0), 0, jnp.maximum(room, 0))
    passed = jax.random.randint(jax.random.fold_in(own, 4), (amount // 2,), 0, 1 << 20) % (room + 1)
    sizes = sizes.at[giver].add(-passed).at[taker].add(passed)
    members = jnp.searchsorted(jnp.cumsum(sizes), jnp.arange(rows * top), side="right").astype(jnp.int32)
    grid = members.reshape(top, rows).T
    grid = grid[jax.random.permutation(jax.random.fold_in(own, 1), rows)]
    turn = jax.random.randint(jax.random.fold_in(own, 2), (rows, 1), 0, top)
    return jnp.take_along_axis(grid, (jnp.arange(top)[None, :] + turn) % top, axis=1)


def load_shares(amount, total, limit, slope, full):
    loads = [(1 << 20) // math.isqrt(standing ** slope) + 1 for standing in range(1, amount + 1)]
    largest = limit if full else min(limit, max(-(-total // amount), total * loads[0] // sum(loads)))
    least = 1 if total - largest >= amount - 1 else 0
    counts, spare = [largest] + [least] * (amount - 1), total - largest - least * (amount - 1)
    while spare > 0:
        candidates = [i for i in range(1, amount) if counts[i] < largest] or [i for i in range(1, amount) if counts[i] < limit]
        mass, remaining = sum([loads[i] for i in candidates]), spare
        for i in candidates:
            extra = min(limit - counts[i], max(1, remaining * loads[i] // mass), spare)
            counts[i] = counts[i] + extra
            spare = spare - extra
    return np.array(counts)


def normal_values(stream_key, dims, spread, bound, cuts=(), kind=jnp.bfloat16):
    drawn = jax.random.normal(stream_key, dims, jnp.float32) * spread
    if len(cuts) > 0:
        drawn = levels(stream_key, dims, cuts, -0.22, 0.18) * drawn
    return jnp.clip(drawn, min=-bound, max=bound).astype(kind)


def setup_inputs(seed: int = 0) -> dict:
    key_of = jax.random.split(jax.random.key(seed), 18)
    x_inner = normal_values(key_of[0], (SEQUENCE_TOKENS, INNER), 1.0, 6.0, ((0, 8), (1, 4)))
    bc_input = normal_values(key_of[1], (SEQUENCE_TOKENS, 2 * STATE), 1.0, 6.0, ((0, 8),))
    gate_input = draw_gate_input(jax.random.fold_in(key_of[17], 71), 0)
    conv_weight = normal_values(key_of[3], (KERNEL, INNER), KERNEL ** -0.5, 3.0, ((1, 4),), jnp.float32)
    bc_conv_weight = normal_values(key_of[4], (KERNEL, 2 * STATE), KERNEL ** -0.5, 3.0, (), jnp.float32)
    step_size = jnp.clip(jnp.exp(math.log(0.05) - 3.218876 * jax.random.uniform(key_of[5], (SEQUENCE_TOKENS, HEADS), jnp.float32) ** levels(key_of[5], (SEQUENCE_TOKENS, HEADS), ((0, 8), (1, 4)), -0.2, 0.2)), 0.002, 0.05)
    log_decay = draw_log_decay(jax.random.fold_in(key_of[17], 71), 0)
    skip_gain = jnp.clip(0.5 + 1.0 * jax.random.uniform(key_of[7], (HEADS,), jnp.float32) ** levels(key_of[7], (HEADS,), ((0, 4),), -0.2, 0.2), 0.5, 1.5)
    norm_gain = jnp.clip(1.0 + 0.15 * jax.random.normal(key_of[8], (INNER,), jnp.float32), 0.25, 1.75)
    out_weight = normal_values(key_of[9], (INNER, D), INNER ** -0.5, 0.09375, ((0, 4),))
    residual = normal_values(key_of[10], (SEQUENCE_TOKENS, D), 1.0, 6.0, ((0, 32),))
    moe_gain = jnp.clip(1.0 + 0.15 * jax.random.normal(key_of[11], (D,), jnp.float32), 0.25, 1.75)
    expert_ids_keys = jax.random.split(jax.random.fold_in(key_of[12], 1), SEQUENCE_TOKENS // TOK_DEV)
    expert_ids_turns = jax.random.permutation(jax.random.fold_in(key_of[12], 3), SEQUENCE_TOKENS // TOK_DEV)
    expert_ids = jax.vmap(lambda own, number: shared_out(jax.random.fold_in(key_of[12], 2), own, number, TOK_DEV, EXPERTS, TOP, CAP, 2))(expert_ids_keys, expert_ids_turns).reshape((SEQUENCE_TOKENS, TOP))
    route_weights = jnp.clip(jnp.exp(math.log(0.6) - 1.7917595 * jax.random.uniform(key_of[13], (SEQUENCE_TOKENS, TOP), jnp.float32) ** levels(key_of[13], (SEQUENCE_TOKENS, TOP), ((0, 32),), -0.2, 0.2)), 0.1, 0.6)
    gate_up_weight = normal_values(key_of[14], (EXPERTS, D, 2 * MOE_FF), D ** -0.5, 0.125, ((0, 4), (1, 8)))
    down_weight = normal_values(key_of[15], (EXPERTS, MOE_FF, D), MOE_FF ** -0.5, 0.21875, ((0, 4), (2, 8)))
    out_grad = normal_values(key_of[16], (SEQUENCE_TOKENS, D), 1.0, 6.0, ((0, 32),))
    return {"x_inner": x_inner, "bc_input": bc_input, "gate_input": gate_input, "conv_weight": conv_weight, "bc_conv_weight": bc_conv_weight, "step_size": step_size, "log_decay": log_decay, "skip_gain": skip_gain, "norm_gain": norm_gain, "out_weight": out_weight, "residual": residual, "moe_gain": moe_gain, "expert_ids": expert_ids, "route_weights": route_weights, "gate_up_weight": gate_up_weight, "down_weight": down_weight, "out_grad": out_grad}


def causal_conv(values, weight):
    kernel_len = weight.shape[0]
    row_total = values.shape[0]
    padded = jnp.pad(values.astype(jnp.float32), ((kernel_len - 1, 0), (0, 0)))
    summed = jnp.zeros((row_total, values.shape[1]), jnp.float32)
    for offset in range(kernel_len):
        summed = summed + weight[offset][None, :] * padded[offset:offset + row_total]
    return summed

def rounded(values):
    return lax.optimization_barrier(values.astype(jnp.bfloat16)).astype(jnp.float32)

def reference(x_inner, bc_input, gate_input, conv_weight, bc_conv_weight, step_size, log_decay, skip_gain, norm_gain, out_weight, residual, moe_gain, expert_ids, route_weights, gate_up_weight, down_weight, out_grad):
    high = lax.Precision.HIGHEST
    conv_x = jax.nn.silu(causal_conv(x_inner, conv_weight)).astype(jnp.bfloat16)
    conv_bc = jax.nn.silu(causal_conv(bc_input, bc_conv_weight)).astype(jnp.bfloat16)
    block_count = SEQUENCE_TOKENS // SPAN
    x_blocks = conv_x.reshape(block_count, SPAN, HEADS, HEAD_DIM)
    b_blocks = conv_bc[:, :STATE].reshape(block_count, SPAN, STATE)
    c_blocks = conv_bc[:, STATE:].reshape(block_count, SPAN, STATE)
    step_blocks = step_size.reshape(block_count, SPAN, HEADS)
    decay_blocks = log_decay.reshape(block_count, SPAN, HEADS)
    causal_mask = (jnp.arange(SPAN)[:, None] >= jnp.arange(SPAN)[None, :])[:, :, None]

    def one_block(held_state, inputs):
        x_block, b_block, c_block, step_block, decay_block = inputs
        cumulative = jnp.cumsum(decay_block, axis=0)
        x_float = x_block.astype(jnp.float32)
        scores = jnp.dot(c_block, b_block.T, preferred_element_type=jnp.float32)
        gap_matrix = cumulative[:, None, :] - cumulative[None, :, :]
        weights = jnp.where(causal_mask, jnp.exp(jnp.where(causal_mask, gap_matrix, 0.0)) * scores[:, :, None] * step_block[None, :, :], 0.0)
        within = jnp.einsum('tsh,shp->thp', rounded(weights), x_float, precision=high)
        entering = rounded(held_state)
        carried = jnp.einsum('tn,hnp->thp', c_block.astype(jnp.float32), entering, precision=high) * jnp.exp(cumulative)[:, :, None]
        tail_scale = jnp.exp(cumulative[-1:, :] - cumulative) * step_block
        scaled_b = rounded(b_block[:, None, :].astype(jnp.float32) * tail_scale[:, :, None])
        block_state = jnp.einsum('lhn,lhp->hnp', scaled_b, x_float, precision=high)
        mixer_out = within + carried + skip_gain[None, :, None] * x_float
        next_state = jnp.exp(cumulative[-1])[:, None, None] * held_state + block_state
        return (next_state, mixer_out)
    last_state, outputs = lax.scan(one_block, jnp.zeros((HEADS, STATE, HEAD_DIM), jnp.float32), (x_blocks, b_blocks, c_blocks, step_blocks, decay_blocks))
    mixer_out = outputs.reshape(SEQUENCE_TOKENS, INNER)
    gated = mixer_out * jax.nn.silu(gate_input.astype(jnp.float32))
    squares = lax.optimization_barrier(jnp.sum(gated * gated, axis=1))
    scaled = (gated * norm_gain[None, :]).astype(jnp.bfloat16)
    group_width = INNER // N_EXP
    summed = jnp.zeros((SEQUENCE_TOKENS, D), jnp.float32)
    for owner_index in range(N_EXP):
        partial_sum = jnp.dot(scaled[:, owner_index * group_width:(owner_index + 1) * group_width], out_weight[owner_index * group_width:(owner_index + 1) * group_width], preferred_element_type=jnp.float32)
        summed = summed + rounded(partial_sum)
    hidden_state = (residual.astype(jnp.float32) + summed * lax.rsqrt(squares / INNER + 1e-05)[:, None]).astype(jnp.bfloat16)
    hidden_f = hidden_state.astype(jnp.float32)
    inv_rms = lax.rsqrt(lax.optimization_barrier(jnp.mean(hidden_f * hidden_f, axis=1)) + 1e-06)
    normed = (hidden_f * inv_rms[:, None] * moe_gain[None, :]).astype(jnp.bfloat16)
    pair_count = SEQUENCE_TOKENS * TOP
    flat_ids = expert_ids.reshape(pair_count).astype(jnp.int32)
    grad_f = out_grad.astype(jnp.float32)
    pair_grads = (route_weights[:, :, None] * grad_f[:, None, :]).astype(jnp.bfloat16).reshape(pair_count, D)
    most_rows = CAP * (SEQUENCE_TOKENS // TOK_DEV)

    def one_expert(carry, inputs):
        outs_all, grads_all = carry
        gu_weight, dn_weight, expert = inputs
        picked = jnp.nonzero(flat_ids == expert, size=most_rows, fill_value=pair_count)[0].astype(jnp.int32)
        safe_index = jnp.minimum(picked, pair_count - 1)
        rows_in = normed[safe_index // TOP]
        projected = jnp.dot(rows_in, gu_weight, preferred_element_type=jnp.float32)
        pre_gate = projected[:, :MOE_FF]
        pre_up = projected[:, MOE_FF:]
        activated = (jax.nn.silu(pre_gate) * pre_up).astype(jnp.bfloat16)
        expert_out = jnp.dot(activated, dn_weight, preferred_element_type=jnp.float32).astype(jnp.bfloat16)
        grads_in = pair_grads[safe_index]
        hidden_grad = jnp.dot(grads_in, dn_weight.T, preferred_element_type=jnp.float32)
        sigmoid_gate = jax.nn.sigmoid(pre_gate)
        grad_gate = hidden_grad * pre_up * sigmoid_gate * (1.0 + pre_gate * (1.0 - sigmoid_gate))
        grad_up = hidden_grad * jax.nn.silu(pre_gate)
        grad_both = jnp.concatenate([grad_gate, grad_up], axis=1).astype(jnp.bfloat16)
        grad_rows = jnp.dot(grad_both, gu_weight.T, preferred_element_type=jnp.float32).astype(jnp.bfloat16)
        outs_all = outs_all.at[picked].set(expert_out, mode='drop')
        grads_all = grads_all.at[picked].set(grad_rows, mode='drop')
        return ((outs_all, grads_all), None)
    start_outs = jnp.zeros((pair_count, D), jnp.bfloat16)
    start_grads = jnp.zeros((pair_count, D), jnp.bfloat16)
    (outs_all, grads_all), unused = lax.scan(one_expert, (start_outs, start_grads), (gate_up_weight, down_weight, jnp.arange(EXPERTS, dtype=jnp.int32)))
    outs_pairs = outs_all.reshape(SEQUENCE_TOKENS, TOP, D).astype(jnp.float32)
    layer_output = (hidden_f + lax.optimization_barrier(jnp.sum(route_weights[:, :, None] * outs_pairs, axis=1))).astype(jnp.bfloat16)
    route_grads = lax.optimization_barrier(jnp.sum(grad_f[:, None, :] * outs_pairs, axis=2))
    normed_grad = lax.optimization_barrier(jnp.sum(grads_all.reshape(SEQUENCE_TOKENS, TOP, D).astype(jnp.float32), axis=1))
    unit_rows = hidden_f * inv_rms[:, None]
    unit_grad = normed_grad * moe_gain[None, :]
    residual_grad = (grad_f + inv_rms[:, None] * (unit_grad - unit_rows * lax.optimization_barrier(jnp.mean(unit_grad * unit_rows, axis=1, keepdims=True)))).astype(jnp.bfloat16)
    return (layer_output, residual_grad, route_grads)
```

```python
import jax
import jax.numpy as jnp
from jax import lax
from jax.sharding import PartitionSpec as P

SPAN = 128
BF = jnp.bfloat16
F32 = jnp.float32


def passed_along(block, axis, distance):
    devices = range(lax.axis_size(axis))
    route = [(i - distance, i) for i in devices if i - distance in devices]
    return lax.ppermute(block, axis, route)


def two_terms(values):
    high = lax.reduce_precision(values, 8, 7)
    return high.astype(BF), (values - high).astype(BF)


def swap(block, axis):
    return lax.all_to_all(block, axis, split_axis=0, concat_axis=0, tiled=True)


def causal_conv(values, weight):
    kernel_len = weight.shape[0]
    row_total = values.shape[0] - kernel_len + 1
    summed = jnp.zeros((row_total, values.shape[1]), F32)
    for offset in range(kernel_len):
        summed = summed + weight[offset][None, :] * values[offset : offset + row_total].astype(F32)
    return summed


def dot(a, b, dims):
    return lax.dot_general(a, b, (dims, ((), ())), preferred_element_type=F32)


def local(
    x_inner,
    bc_input,
    gate_input,
    conv_weight,
    bc_conv_weight,
    step_size,
    log_decay,
    skip_gain,
    norm_gain,
    out_weight,
    residual,
    moe_gain,
    expert_ids,
    route_weights,
    gate_up_weight,
    down_weight,
    out_grad,
):
    ctx, owners = lax.axis_size("ctx"), lax.axis_size("exp")
    local_count = gate_up_weight.shape[0]
    expert_total = local_count * owners
    full_gu, full_down = [], []
    for j in range(local_count):
        full_gu.append(lax.all_gather(gate_up_weight[j], "ctx", axis=0, tiled=True))
        full_down.append(lax.all_gather(down_weight[j], "ctx", axis=1, tiled=True))
    ff_width = down_weight.shape[1]

    tok_rows, model_width = residual.shape
    top_count = expert_ids.shape[1]
    onehot = expert_ids[:, :, None] == jnp.arange(expert_total, dtype=jnp.int32)[None, None, :]
    dense_route = jnp.sum(jnp.where(onehot, route_weights[:, :, None], 0.0), axis=1)
    owned = dense_route.reshape(tok_rows, owners, local_count).transpose(1, 0, 2)
    pad = jnp.zeros((owners, tok_rows, 128 - 2 * local_count), BF)
    grads_sent = jnp.concatenate(
        [
            jnp.broadcast_to(out_grad[None], (owners, tok_rows, model_width)),
            *two_terms(owned),
            pad,
        ],
        axis=2,
    )
    grads_here = swap(grads_sent, "exp").reshape(owners * tok_rows, model_width + 128)
    all_grads = grads_here[:, :model_width]
    route_here = grads_here[:, model_width : model_width + 2 * local_count].astype(F32)
    route_here = route_here[:, :local_count] + route_here[:, local_count:]

    kernel_len = conv_weight.shape[0]
    row_count, channel_count = x_inner.shape
    head_count = step_size.shape[1]
    state_size = bc_input.shape[1] // 2
    head_width = channel_count // head_count
    joined = jnp.concatenate([x_inner, bc_input], axis=1)
    rim_rows = passed_along(joined[row_count - kernel_len + 1 :], "ctx", 1)
    padded = jnp.concatenate([rim_rows, joined], axis=0)
    joint_weight = jnp.concatenate([conv_weight, bc_conv_weight], axis=1)
    convolved = jax.nn.silu(causal_conv(padded, joint_weight)).astype(BF)
    conv_x = convolved[:, :channel_count]
    conv_b = convolved[:, channel_count : channel_count + state_size]
    conv_c = convolved[:, channel_count + state_size :]
    block_count = row_count // SPAN
    x_blocks = conv_x.reshape(block_count, SPAN, head_count, head_width)
    b_blocks = conv_b.reshape(block_count, SPAN, state_size)
    c_blocks = conv_c.reshape(block_count, SPAN, state_size)
    step_blocks = step_size.reshape(block_count, SPAN, head_count)
    decay_blocks = log_decay.reshape(block_count, SPAN, head_count)
    cumulative = jnp.cumsum(decay_blocks, axis=1)

    def wide(per_head):
        shape = per_head.shape
        return jnp.broadcast_to(per_head[..., None], (*shape, head_width)).reshape(
            *shape[:-1], channel_count
        )

    tail_scale = jnp.exp(cumulative[:, -1:, :] - cumulative) * step_blocks
    scaled_x = (
        x_blocks.reshape(block_count, SPAN, channel_count).astype(F32) * wide(tail_scale)
    ).astype(BF)
    states = jnp.einsum("cln,clq->cnq", b_blocks, scaled_x, preferred_element_type=F32)
    block_decay = wide(jnp.exp(cumulative[:, -1, :]))
    held = jnp.zeros((state_size, channel_count), F32)
    factor = jnp.ones((channel_count,), F32)
    local_in, factor_in = [], []
    for j in range(block_count):
        local_in.append(held)
        factor_in.append(factor)
        held = block_decay[j][None, :] * held + states[j]
        factor = factor * block_decay[j]
    part = state_size // ctx
    factor_terms = jnp.concatenate(
        [*(t[None, None, :] for t in two_terms(factor)), jnp.zeros((1, 14, channel_count), BF)],
        axis=1,
    )
    state_sent = jnp.concatenate(
        [
            held.astype(BF).reshape(ctx, part, channel_count),
            jnp.broadcast_to(factor_terms, (ctx, 16, channel_count)),
        ],
        axis=1,
    )
    state_here = swap(state_sent, "ctx").astype(F32)
    running = jnp.zeros((part, channel_count), F32)
    prefixes = []
    for i in range(ctx):
        prefixes.append(running.astype(BF))
        decay_i = state_here[i, part] + state_here[i, part + 1]
        running = decay_i[None, :] * running + state_here[i, :part]
    arriving = swap(jnp.stack(prefixes), "ctx").reshape(state_size, channel_count).astype(F32)

    scores = jnp.einsum("ctn,csn->cts", c_blocks, b_blocks, preferred_element_type=F32)
    causal_mask = (jnp.arange(SPAN)[:, None] >= jnp.arange(SPAN)[None, :])[None, None, :, :]
    cum_h = cumulative.transpose(0, 2, 1)
    step_h = step_blocks.transpose(0, 2, 1)
    gap_matrix = cum_h[:, :, :, None] - cum_h[:, :, None, :]
    weights = jnp.where(
        causal_mask,
        jnp.exp(jnp.where(causal_mask, gap_matrix, 0.0))
        * scores[:, None]
        * step_h[:, :, None, :],
        0.0,
    ).astype(BF)
    within = jnp.einsum("chts,cshp->cthp", weights, x_blocks, preferred_element_type=F32)
    entering = jnp.stack(
        [
            (local_in[j] + factor_in[j][None, :] * arriving).astype(BF)
            for j in range(block_count)
        ]
    )
    carried = jnp.einsum("ctn,cnq->ctq", c_blocks, entering, preferred_element_type=F32) * wide(
        jnp.exp(cumulative)
    )
    mixer_out = (
        within.reshape(row_count, channel_count)
        + carried.reshape(row_count, channel_count)
        + wide(skip_gain)[None, :] * conv_x.astype(F32)
    )
    gated = mixer_out * jax.nn.silu(gate_input.astype(F32))
    squares = jnp.sum(gated * gated, axis=1)
    scaled = (gated * norm_gain[None, :]).astype(BF)
    projected_rows = jnp.dot(scaled, out_weight, preferred_element_type=F32).astype(BF)
    mixed_sent = jnp.concatenate(
        [
            projected_rows,
            *(t[:, None] for t in two_terms(squares)),
            jnp.zeros((row_count, 126), BF),
        ],
        axis=1,
    ).reshape(owners, tok_rows, model_width + 128)
    mixed = jnp.sum(swap(mixed_sent, "exp").astype(F32), axis=0)
    mixed_rows = mixed[:, :model_width]
    own_squares = mixed[:, model_width] + mixed[:, model_width + 1]
    inner_total = channel_count * owners
    hidden_state = (
        residual.astype(F32)
        + mixed_rows * lax.rsqrt(own_squares / inner_total + 1e-05)[:, None]
    ).astype(BF)
    hidden_f = hidden_state.astype(F32)
    inv_rms = lax.rsqrt(jnp.mean(hidden_f * hidden_f, axis=1) + 1e-06)
    normed = (hidden_f * inv_rms[:, None] * moe_gain[None, :]).astype(BF)
    all_normed = swap(
        jnp.broadcast_to(normed[None], (owners, tok_rows, model_width)), "exp"
    ).reshape(owners * tok_rows, model_width)

    out_part = jnp.zeros((owners * tok_rows, model_width), F32)
    grad_part = jnp.zeros((owners * tok_rows, model_width), F32)
    route_part = []
    for j in range(local_count):
        route = route_here[:, j : j + 1]
        projected = dot(all_normed, full_gu[j], ((1,), (0,)))
        pre_gate, pre_up = projected[:, :ff_width], projected[:, ff_width:]
        hidden_grad = dot(all_grads, full_down[j], ((1,), (1,)))
        gate = jax.nn.sigmoid(pre_gate)
        silu_gate = pre_gate * gate
        activated = silu_gate * pre_up
        route_part.append(jnp.sum(activated * hidden_grad, axis=1))
        hidden_grad = hidden_grad * route
        grad_both = jnp.concatenate(
            [
                hidden_grad * pre_up * gate * (1.0 + pre_gate * (1.0 - gate)),
                hidden_grad * silu_gate,
            ],
            axis=1,
        ).astype(BF)
        out_part = out_part + dot((activated * route).astype(BF), full_down[j], ((1,), (0,)))
        grad_part = grad_part + dot(grad_both, full_gu[j], ((1,), (1,)))
    route_terms = two_terms(jnp.stack(route_part, axis=1))
    out_sent = jnp.concatenate(
        [
            out_part.astype(BF),
            *route_terms,
            jnp.zeros((owners * tok_rows, 128 - 2 * local_count), BF),
        ],
        axis=1,
    ).reshape(owners, tok_rows, model_width + 128)
    out_here = swap(out_sent, "exp").astype(F32)
    grad_here = swap(grad_part.astype(BF).reshape(owners, tok_rows, model_width), "exp")
    layer_output = (hidden_f + jnp.sum(out_here[:, :, :model_width], axis=0)).astype(BF)
    route_all = (
        out_here[:, :, model_width : model_width + local_count]
        + out_here[:, :, model_width + local_count : model_width + 2 * local_count]
    )
    route_all = route_all.transpose(1, 0, 2).reshape(tok_rows, 1, expert_total)
    route_grads = jnp.sum(jnp.where(onehot, route_all, 0.0), axis=2)
    normed_grad = jnp.sum(grad_here.astype(F32), axis=0)
    unit_rows = hidden_f * inv_rms[:, None]
    unit_grad = normed_grad * moe_gain[None, :]
    residual_grad = (
        out_grad.astype(F32)
        + inv_rms[:, None]
        * (unit_grad - unit_rows * jnp.mean(unit_grad * unit_rows, axis=1, keepdims=True))
    ).astype(BF)
    return (layer_output, residual_grad, route_grads)


def solution(mesh):
    return jax.shard_map(
        local,
        mesh=mesh,
        in_specs=(
            P("ctx", "exp"),
            P("ctx", None),
            P("ctx", "exp"),
            P(None, "exp"),
            P(),
            P("ctx", "exp"),
            P("ctx", "exp"),
            P("exp"),
            P("exp"),
            P("exp", None),
            P(("ctx", "exp"), None),
            P(),
            P(("ctx", "exp"), None),
            P(("ctx", "exp"), None),
            P("exp", "ctx", None),
            P("exp", None, "ctx"),
            P(("ctx", "exp"), None),
        ),
        out_specs=(P(("ctx", "exp"), None), P(("ctx", "exp"), None), P(("ctx", "exp"), None)),
        check_vma=False,
    )
```

```python
import functools

import jax
import jax.numpy as jnp
from jax import lax
from jax.experimental import pallas as pl
from jax.experimental.pallas import tpu as pltpu
from jax.sharding import PartitionSpec as P

SPAN = 128
BF = jnp.bfloat16
F32 = jnp.float32


def passed_along(block, axis, distance):
    devices = range(lax.axis_size(axis))
    route = [(i - distance, i) for i in devices if i - distance in devices]
    return lax.ppermute(block, axis, route)


def two_terms(values):
    high = lax.reduce_precision(values, 8, 7)
    return high.astype(BF), (values - high).astype(BF)


def swap(block, axis):
    return lax.all_to_all(block, axis, split_axis=0, concat_axis=0, tiled=True)


def causal_conv(values, weight):
    kernel_len = weight.shape[0]
    row_total = values.shape[0] - kernel_len + 1
    summed = jnp.zeros((row_total, values.shape[1]), F32)
    for offset in range(kernel_len):
        summed = summed + weight[offset][None, :] * values[offset : offset + row_total].astype(F32)
    return summed


def dot(a, b, dims):
    return lax.dot_general(a, b, (dims, ((), ())), preferred_element_type=F32)


def chip_ring(chips):
    return [0, *range(1, chips, 2), *[c for c in range(chips - 1, 0, -1) if c % 2 == 0]]


def gathered(shard, order):
    chips = len(order)
    along = [
        (2 * order[t] + core, 2 * order[(t + 1) % chips] + core)
        for t in range(chips)
        for core in range(2)
    ]
    across = [(i, i ^ 1) for i in range(2 * chips)]
    held, slots = shard, []
    for step in range(chips):
        later = lax.ppermute(held, "ctx", along) if step < chips - 1 else None
        slots += [held, lax.ppermute(held, "ctx", across)]
        held = later
    return slots


def experts_kernel(count, width, places, x_ref, g_ref, route_ref, *refs):
    gus, downs = refs[:count], refs[count : 2 * count]
    out_ref, grad_ref, pair_ref, out_acc, grad_acc = refs[2 * count :]
    depth = gus[0].shape[1]
    columns = [pl.ds(pl.multiple_of(places[k] * depth, depth), depth) for k in range(count)]
    pair_ref[...] = jnp.zeros_like(pair_ref)
    for j in range(gus[0].shape[0]):
        projected = dot(x_ref[:, columns[0]], gus[0][j], ((1,), (0,)))
        hidden_grad = dot(g_ref[:, columns[0]], downs[0][j], ((1,), (1,)))
        for k in range(1, count):
            projected += dot(x_ref[:, columns[k]], gus[k][j], ((1,), (0,)))
            hidden_grad += dot(g_ref[:, columns[k]], downs[k][j], ((1,), (1,)))
        route = route_ref[:, j : j + 1]
        pre_gate, pre_up = projected[:, :width], projected[:, width:]
        gate = jax.nn.sigmoid(pre_gate)
        silu_gate = pre_gate * gate
        activated = silu_gate * pre_up
        pair_ref[:, j : j + 1] = jnp.sum(activated * hidden_grad, axis=1, keepdims=True)
        hidden_grad = hidden_grad * route
        grad_both = jnp.concatenate(
            [
                hidden_grad * pre_up * gate * (1.0 + pre_gate * (1.0 - gate)),
                hidden_grad * silu_gate,
            ],
            axis=1,
        ).astype(BF)
        activated = (activated * route).astype(BF)
        for k in range(count):
            out_k = dot(activated, downs[k][j], ((1,), (0,)))
            grad_k = dot(grad_both, gus[k][j], ((1,), (1,)))
            if j > 0:
                out_k += out_acc[:, columns[k]]
                grad_k += grad_acc[:, columns[k]]
            if j < gus[0].shape[0] - 1:
                out_acc[:, columns[k]] = out_k
                grad_acc[:, columns[k]] = grad_k
            else:
                out_ref[:, columns[k]] = out_k.astype(BF)
                grad_ref[:, columns[k]] = grad_k.astype(BF)


def experts(places, x, g, route, gus, downs):
    rows, model_width = x.shape
    tile, count, width = 256, len(gus), downs[0].shape[1]

    def whole(a):
        return pl.BlockSpec(a.shape, lambda i: (0, 0, 0), pipeline_mode=pl.Buffered(1))

    wide_rows = pl.BlockSpec((tile, model_width), lambda i: (i, 0))
    lane_rows = pl.BlockSpec((tile, 128), lambda i: (i, 0))
    flops = 12 * rows * model_width * width * gus[0].shape[0]
    return pl.pallas_call(
        functools.partial(experts_kernel, count, width),
        grid=(rows // tile,),
        in_specs=[
            pl.BlockSpec(memory_space=pltpu.SMEM),
            wide_rows,
            wide_rows,
            lane_rows,
            *[whole(a) for a in gus],
            *[whole(a) for a in downs],
        ],
        out_specs=[wide_rows, wide_rows, lane_rows],
        out_shape=[
            jax.ShapeDtypeStruct((rows, model_width), BF),
            jax.ShapeDtypeStruct((rows, model_width), BF),
            jax.ShapeDtypeStruct((rows, 128), F32),
        ],
        scratch_shapes=[pltpu.VMEM((tile, model_width), F32)] * 2,
        compiler_params=pltpu.CompilerParams(vmem_limit_bytes=56 * 2**20),
        cost_estimate=pl.CostEstimate(
            flops=flops, bytes_accessed=24 * 2**20, transcendentals=rows * width
        ),
    )(places, x, g, route, *gus, *downs)


def local(
    x_inner,
    bc_input,
    gate_input,
    conv_weight,
    bc_conv_weight,
    step_size,
    log_decay,
    skip_gain,
    norm_gain,
    out_weight,
    residual,
    moe_gain,
    expert_ids,
    route_weights,
    gate_up_weight,
    down_weight,
    out_grad,
):
    ctx, owners = lax.axis_size("ctx"), lax.axis_size("exp")
    local_count = gate_up_weight.shape[0]
    expert_total = local_count * owners
    order = chip_ring(ctx // 2)
    place = lax.axis_index("ctx")
    chip, core = place // 2, place % 2
    ring_place = jnp.array([order.index(c) for c in range(ctx // 2)], jnp.int32)[chip]
    sources = jnp.array(order, jnp.int32)[
        (ring_place - jnp.arange(ctx // 2, dtype=jnp.int32)) % (ctx // 2)
    ]
    places = jnp.stack([2 * sources + core, 2 * sources + 1 - core], axis=1).reshape(ctx)
    gus = gathered(gate_up_weight, order)
    downs = gathered(down_weight, order)

    tok_rows, model_width = residual.shape
    top_count = expert_ids.shape[1]
    onehot = expert_ids[:, :, None] == jnp.arange(expert_total, dtype=jnp.int32)[None, None, :]
    dense_route = jnp.sum(jnp.where(onehot, route_weights[:, :, None], 0.0), axis=1)
    owned = dense_route.reshape(tok_rows, owners, local_count).transpose(1, 0, 2)
    kernel_len = conv_weight.shape[0]
    row_count, channel_count = x_inner.shape
    head_count = step_size.shape[1]
    state_size = bc_input.shape[1] // 2
    head_width = channel_count // head_count
    joined = jnp.concatenate([x_inner, bc_input], axis=1)
    rim_rows = passed_along(joined[row_count - kernel_len + 1 :], "ctx", 1)
    padded = jnp.concatenate([rim_rows, joined], axis=0)
    joint_weight = jnp.concatenate([conv_weight, bc_conv_weight], axis=1)
    convolved = jax.nn.silu(causal_conv(padded, joint_weight)).astype(BF)
    conv_x = convolved[:, :channel_count]
    conv_b = convolved[:, channel_count : channel_count + state_size]
    conv_c = convolved[:, channel_count + state_size :]
    block_count = row_count // SPAN
    x_blocks = conv_x.reshape(block_count, SPAN, head_count, head_width)
    b_blocks = conv_b.reshape(block_count, SPAN, state_size)
    c_blocks = conv_c.reshape(block_count, SPAN, state_size)
    step_blocks = step_size.reshape(block_count, SPAN, head_count)
    decay_blocks = log_decay.reshape(block_count, SPAN, head_count)
    cumulative = jnp.cumsum(decay_blocks, axis=1)

    def wide(per_head):
        shape = per_head.shape
        return jnp.broadcast_to(per_head[..., None], (*shape, head_width)).reshape(
            *shape[:-1], channel_count
        )

    tail_scale = jnp.exp(cumulative[:, -1:, :] - cumulative) * step_blocks
    scaled_x = (
        x_blocks.reshape(block_count, SPAN, channel_count).astype(F32) * wide(tail_scale)
    ).astype(BF)
    states = jnp.einsum("cln,clq->cnq", b_blocks, scaled_x, preferred_element_type=F32)
    block_decay = wide(jnp.exp(cumulative[:, -1, :]))
    held = jnp.zeros((state_size, channel_count), F32)
    factor = jnp.ones((channel_count,), F32)
    local_in, factor_in = [], []
    for j in range(block_count):
        local_in.append(held)
        factor_in.append(factor)
        held = block_decay[j][None, :] * held + states[j]
        factor = factor * block_decay[j]
    part = state_size // ctx
    factor_terms = jnp.concatenate(
        [*(t[None, None, :] for t in two_terms(factor)), jnp.zeros((1, 14, channel_count), BF)],
        axis=1,
    )
    state_sent = jnp.concatenate(
        [
            held.astype(BF).reshape(ctx, part, channel_count),
            jnp.broadcast_to(factor_terms, (ctx, 16, channel_count)),
        ],
        axis=1,
    )
    state_here = swap(state_sent, "ctx").astype(F32)
    running = jnp.zeros((part, channel_count), F32)
    prefixes = []
    for i in range(ctx):
        prefixes.append(running.astype(BF))
        decay_i = state_here[i, part] + state_here[i, part + 1]
        running = decay_i[None, :] * running + state_here[i, :part]
    arriving = swap(jnp.stack(prefixes), "ctx").reshape(state_size, channel_count).astype(F32)

    scores = jnp.einsum("ctn,csn->cts", c_blocks, b_blocks, preferred_element_type=F32)
    causal_mask = (jnp.arange(SPAN)[:, None] >= jnp.arange(SPAN)[None, :])[None, None, :, :]
    cum_h = cumulative.transpose(0, 2, 1)
    step_h = step_blocks.transpose(0, 2, 1)
    gap_matrix = cum_h[:, :, :, None] - cum_h[:, :, None, :]
    weights = jnp.where(
        causal_mask,
        jnp.exp(jnp.where(causal_mask, gap_matrix, 0.0))
        * scores[:, None]
        * step_h[:, :, None, :],
        0.0,
    ).astype(BF)
    within = jnp.einsum("chts,cshp->cthp", weights, x_blocks, preferred_element_type=F32)
    entering = jnp.stack(
        [
            (local_in[j] + factor_in[j][None, :] * arriving).astype(BF)
            for j in range(block_count)
        ]
    )
    carried = jnp.einsum("ctn,cnq->ctq", c_blocks, entering, preferred_element_type=F32) * wide(
        jnp.exp(cumulative)
    )
    mixer_out = (
        within.reshape(row_count, channel_count)
        + carried.reshape(row_count, channel_count)
        + wide(skip_gain)[None, :] * conv_x.astype(F32)
    )
    gated = mixer_out * jax.nn.silu(gate_input.astype(F32))
    squares = jnp.sum(gated * gated, axis=1)
    scaled = (gated * norm_gain[None, :]).astype(BF)
    projected_rows = jnp.dot(scaled, out_weight, preferred_element_type=F32).astype(BF)
    mixed_sent = jnp.concatenate(
        [
            projected_rows,
            *(t[:, None] for t in two_terms(squares)),
            jnp.zeros((row_count, 126), BF),
        ],
        axis=1,
    ).reshape(owners, tok_rows, model_width + 128)
    mixed_back = swap(mixed_sent, "exp")
    pad = jnp.zeros((owners, tok_rows, 128 - 2 * local_count), BF)
    out_grad_late, mixed_back = lax.optimization_barrier((out_grad, mixed_back))
    grads_sent = jnp.concatenate(
        [
            jnp.broadcast_to(out_grad_late[None], (owners, tok_rows, model_width)),
            *two_terms(owned),
            pad,
        ],
        axis=2,
    )
    grads_here = swap(grads_sent, "exp").reshape(owners * tok_rows, model_width + 128)
    all_grads = grads_here[:, :model_width]
    route_here = grads_here[:, model_width : model_width + 2 * local_count].astype(F32)
    route_here = route_here[:, :local_count] + route_here[:, local_count:]
    route_here = jnp.pad(route_here, ((0, 0), (0, 128 - local_count)))

    mixed = jnp.sum(mixed_back.astype(F32), axis=0)
    mixed_rows = mixed[:, :model_width]
    own_squares = mixed[:, model_width] + mixed[:, model_width + 1]
    inner_total = channel_count * owners
    hidden_state = (
        residual.astype(F32)
        + mixed_rows * lax.rsqrt(own_squares / inner_total + 1e-05)[:, None]
    ).astype(BF)
    hidden_f = hidden_state.astype(F32)
    inv_rms = lax.rsqrt(jnp.mean(hidden_f * hidden_f, axis=1) + 1e-06)
    normed = (hidden_f * inv_rms[:, None] * moe_gain[None, :]).astype(BF)
    all_normed = swap(
        jnp.broadcast_to(normed[None], (owners, tok_rows, model_width)), "exp"
    ).reshape(owners * tok_rows, model_width)

    out_part, grad_part, route_part = experts(
        places, all_normed, all_grads, route_here, gus, downs
    )
    route_terms = two_terms(route_part[:, :local_count])
    out_sent = jnp.concatenate(
        [
            out_part,
            *route_terms,
            jnp.zeros((owners * tok_rows, 128 - 2 * local_count), BF),
        ],
        axis=1,
    ).reshape(owners, tok_rows, model_width + 128)
    out_here = swap(out_sent, "exp").astype(F32)
    grad_here = swap(grad_part.reshape(owners, tok_rows, model_width), "exp")
    layer_output = (hidden_f + jnp.sum(out_here[:, :, :model_width], axis=0)).astype(BF)
    route_all = (
        out_here[:, :, model_width : model_width + local_count]
        + out_here[:, :, model_width + local_count : model_width + 2 * local_count]
    )
    route_all = route_all.transpose(1, 0, 2).reshape(tok_rows, 1, expert_total)
    route_grads = jnp.sum(jnp.where(onehot, route_all, 0.0), axis=2)
    normed_grad = jnp.sum(grad_here.astype(F32), axis=0)
    unit_rows = hidden_f * inv_rms[:, None]
    unit_grad = normed_grad * moe_gain[None, :]
    residual_grad = (
        out_grad.astype(F32)
        + inv_rms[:, None]
        * (unit_grad - unit_rows * jnp.mean(unit_grad * unit_rows, axis=1, keepdims=True))
    ).astype(BF)
    return (layer_output, residual_grad, route_grads)


def solution(mesh):
    return jax.shard_map(
        local,
        mesh=mesh,
        in_specs=(
            P("ctx", "exp"),
            P("ctx", None),
            P("ctx", "exp"),
            P(None, "exp"),
            P(),
            P("ctx", "exp"),
            P("ctx", "exp"),
            P("exp"),
            P("exp"),
            P("exp", None),
            P(("ctx", "exp"), None),
            P(),
            P(("ctx", "exp"), None),
            P(("ctx", "exp"), None),
            P("exp", "ctx", None),
            P("exp", None, "ctx"),
            P(("ctx", "exp"), None),
        ),
        out_specs=(P(("ctx", "exp"), None), P(("ctx", "exp"), None), P(("ctx", "exp"), None)),
        check_vma=False,
    )
```
